32 devices in a mesh: patch: 16 (over z, y, core), head: 2 (over x).
Axes of the slice: x: 2, y: 2, z: 4, core: 2. Of those that a mesh axis runs over, the one named last changes fastest.
Arguments:
- hidden_states: bfloat16 [2048, 3072], P('patch', 'head'), may hold values from -500 to 500, as said below
- shift_mod: float32 [3072], replicated, may hold values from -3 to 3
- scale_mod: float32 [3072], replicated, may hold values from -3 to 3
- gate_mod: float32 [3072], P('head'), may hold values from 1 to 6
- qkv_weight: bfloat16 [3072, 3, 2048], P('patch', None, 'head'), may hold values from -0.109375 to 0.109375
- query_gain: float32 [128], replicated, may hold values from 1 to 2.5
- key_gain: float32 [128], replicated, may hold values from 1 to 2.5
- text_keys: bfloat16 [512, 2048], P(None, 'head'), may hold values from -6 to 6
- text_values: bfloat16 [512, 2048], P(None, 'head'), may hold values from -6 to 6
- stale_keys: bfloat16 [2048, 2048], P('patch', 'head'), may hold values from -330 to 330, as said below
- stale_values: bfloat16 [2048, 2048], P('patch', 'head'), may hold values from -6 to 6
- out_weight: bfloat16 [2048, 3072], P('head'), may hold values from -0.125 to 0.125
Outputs:
- update: bfloat16 [2048, 3072], P('patch', 'head')
The draws below stay inside these ranges and needn't reach their ends.
Inputs may be any that keep to these rules, and one draw needn't show every extreme that they name: `hidden_states`: finite real values. `stale_keys`: finite real values.
All inputs are finite; a program needn't handle non-finite values.
Results may differ from the reference program's by a relative error of at most 0.02.
The reference program's roundings to bfloat16 on the way (of `modulated`, `weights` and `attention`) count: a program that leaves them out, or rounds other values in their place, can miss the bound.
Values may be sent and summed in bfloat16 or wider, within the bound.
No kernel may reach another device: no remote copies, remote signals or barrier semaphores. Data moves between devices by JAX's collectives and lax.ppermute only.
A program may use at most 128 MiB of HBM per device.

```python
import math
import jax
import jax.numpy as jnp
from jax import lax

D = 3072
HEADS = 16
HD = 128
TXT = 512
TOK_DEV = 128
TOKENS = 2048
N_PATCH = 16


def draw_hidden_states(key, part):
    key = jax.random.fold_in(key, 11)
    base_key, row_key, col_key = jax.random.split(key, 3)
    row_scale = jnp.exp(jax.random.uniform(row_key, (TOKENS, 1), jnp.float32) * math.log(10.0))
    col_scale = jnp.exp(jax.random.uniform(col_key, (1, D), jnp.float32) * math.log(10.0))
    base = jnp.clip(jax.random.normal(base_key, (TOKENS, D), jnp.float32), -4.0, 4.0)
    return (base * row_scale * col_scale).astype(jnp.bfloat16)


def draw_stale_keys(key, part):
    key = jax.random.fold_in(key, 23)
    base_key = jax.random.fold_in(key, 0)
    shape = (TOKENS, HEADS * HD)
    base = jnp.clip(jax.random.normal(base_key, shape, jnp.float32), -4.0, 4.0) * 1.5
    return base.astype(jnp.bfloat16)


def block_scale(own_key, shape, shards, smallest, high):
    factor_of = 1.0
    for dim, parts in shards:
        draws = jax.random.uniform(jax.random.fold_in(jax.random.fold_in(own_key, 6), dim), (parts,), jnp.float32, smallest / len(shards), high / len(shards))
        factor_of = factor_of * jnp.repeat(jnp.exp(draws), shape[dim] // parts).reshape((-1,) + (1,) * (len(shape) - 1 - dim))
    return factor_of


def noise(rng, extent, scale, bound, shards=(), kind=jnp.bfloat16):
    drawn = jax.random.normal(rng, extent, jnp.float32) * scale
    if len(shards) > 0:
        drawn = block_scale(rng, extent, shards, -0.22, 0.18) * drawn
    return jnp.clip(drawn, min=-bound, max=bound).astype(kind)


def setup_inputs(seed: int = 0) -> dict:
    seeds = jax.random.split(jax.random.key(seed), 13)
    return {
        "hidden_states": draw_hidden_states(jax.random.fold_in(seeds[12], 71), 0),
        "shift_mod": noise(seeds[1], (D,), 0.5, 3.0, (), jnp.float32),
        "scale_mod": noise(seeds[2], (D,), 0.5, 3.0, (), jnp.float32),
        "gate_mod": jnp.clip(jnp.exp(math.log(6.0) - 1.7917595 * jax.random.uniform(seeds[3], (D,), jnp.float32) ** block_scale(seeds[3], (D,), ((0, 2),), -0.2, 0.2)), 1.0, 6.0),
        "qkv_weight": noise(seeds[4], (D, 3, HEADS * HD), D ** -0.5, 0.109375, ((0, 16), (2, 2))),
        "query_gain": jnp.clip(jnp.exp(jax.random.uniform(seeds[5], (HD,), jnp.float32, math.log(1.0), math.log(2.5))), 1.0, 2.5),
        "key_gain": jnp.clip(jnp.exp(jax.random.uniform(seeds[6], (HD,), jnp.float32, math.log(1.0), math.log(2.5))), 1.0, 2.5),
        "text_keys": noise(seeds[7], (TXT, HEADS * HD), 1.5, 6.0, ((1, 2),)),
        "text_values": noise(seeds[8], (TXT, HEADS * HD), 1.0, 6.0, ((1, 2),)),
        "stale_keys": draw_stale_keys(jax.random.fold_in(seeds[12], 71), 0),
        "stale_values": noise(seeds[10], (TOKENS, HEADS * HD), 1.0, 6.0, ((0, 16), (1, 2))),
        "out_weight": noise(seeds[11], (HEADS * HD, D), (HEADS * HD) ** -0.5, 0.125, ((0, 2),)),
    }


def head_norm(raw, gain):
    power = lax.optimization_barrier(jnp.mean(raw * raw, axis=-1, keepdims=True))
    return raw * lax.rsqrt(power + 1e-06) * gain

def reference(hidden_states, shift_mod, scale_mod, gate_mod, qkv_weight, query_gain, key_gain, text_keys, text_values, stale_keys, stale_values, out_weight):
    widths = HEADS * HD
    states = hidden_states.astype(jnp.float32)
    center = lax.optimization_barrier(jnp.mean(states, axis=-1, keepdims=True))
    spread = lax.optimization_barrier(jnp.mean((states - center) ** 2, axis=-1, keepdims=True))
    normed = (states - center) * lax.rsqrt(spread + 1e-06)
    modulated = ((1.0 + scale_mod) * normed + shift_mod).astype(jnp.bfloat16)
    projected = jnp.dot(modulated, qkv_weight.reshape(D, 3 * widths), preferred_element_type=jnp.float32)
    projected = projected.reshape(TOKENS, 3, HEADS, HD)
    queries = head_norm(projected[:, 0], query_gain).astype(jnp.bfloat16)
    fresh_keys = head_norm(projected[:, 1], key_gain).astype(jnp.bfloat16).reshape(TOKENS, widths)
    fresh_values = projected[:, 2].astype(jnp.bfloat16).reshape(TOKENS, widths)
    factor = HD ** (-0.5)

    def per_patch(index):
        begin = (index * TOK_DEV).astype(jnp.int32)
        zero = jnp.zeros((), jnp.int32)
        query_block = lax.dynamic_slice_in_dim(queries, begin, TOK_DEV, 0)
        own_keys = lax.dynamic_slice_in_dim(fresh_keys, begin, TOK_DEV, 0)
        own_values = lax.dynamic_slice_in_dim(fresh_values, begin, TOK_DEV, 0)
        image_keys = lax.dynamic_update_slice(stale_keys, own_keys, (begin, zero))
        image_values = lax.dynamic_update_slice(stale_values, own_values, (begin, zero))
        all_keys = jnp.concatenate([text_keys, image_keys], axis=0).reshape(TXT + TOKENS, HEADS, HD)
        all_values = jnp.concatenate([text_values, image_values], axis=0).reshape(TXT + TOKENS, HEADS, HD)
        scores = jnp.einsum('qhd,khd->hqk', query_block.astype(jnp.float32), all_keys.astype(jnp.float32)) * factor
        peak = lax.optimization_barrier(jnp.max(scores, axis=-1, keepdims=True))
        exps = jnp.exp(scores - peak)
        totals = lax.optimization_barrier(jnp.sum(exps, axis=-1))
        weights = exps.astype(jnp.bfloat16).astype(jnp.float32)
        mixed = jnp.einsum('hqk,khd->qhd', weights, all_values.astype(jnp.float32))
        result = mixed / jnp.transpose(totals)[:, :, None]
        return result.astype(jnp.bfloat16).reshape(TOK_DEV, widths)
    attention = lax.map(per_patch, jnp.arange(N_PATCH, dtype=jnp.int32)).reshape(TOKENS, widths)
    summed = jnp.dot(attention, out_weight, preferred_element_type=jnp.float32)
    return (summed * gate_mod).astype(jnp.bfloat16)
```

```python
import functools
import math

import jax
import jax.numpy as jnp
from jax import lax
from jax.experimental import pallas as pl
from jax.experimental.pallas import tpu as pltpu
from jax.sharding import Mesh
from jax.sharding import PartitionSpec as P

ANY = pl.BlockSpec(memory_space=pl.ANY)
VMEM = pl.BlockSpec(memory_space=pltpu.VMEM)
MIB = 1024 * 1024
ACROSS = (((1,), (1,)), ((), ()))


def params(limit):
    return pltpu.CompilerParams(vmem_limit_bytes=limit * MIB)


def column(index, width):
    return pl.ds(pl.multiple_of(index * width, 128), width)


def gray(place):
    return place ^ (place >> 1)


def group_at(step, groups):
    return gray(lax.rem(gray(lax.axis_index("group")) + (step + groups), groups))


def pack_kernel(groups, weight, keys, values, *refs):
    outs, sems = refs[:-1], refs[-1]
    started = []
    for step in range(groups):
        rows, pair = outs[step], outs[groups + step]
        cols = column(group_at(step, groups), rows.shape[2])
        copies = [(weight.at[:, :, cols], rows)]
        copies += [(keys.at[:, cols], pair.at[0]), (values.at[:, cols], pair.at[1])]
        for index, (source, target) in enumerate(copies):
            copy = pltpu.make_async_copy(source, target, sems.at[step, index])
            copy.start()
            started.append(copy)
    for copy in started:
        copy.wait()


def pack(weight, keys, values, groups):
    parts, depth, full = weight.shape
    tok, width = keys.shape[0], full // groups
    rows = jax.ShapeDtypeStruct((parts, depth, width), jnp.bfloat16)
    pair = jax.ShapeDtypeStruct((2, tok, width), jnp.bfloat16)
    outs = pl.pallas_call(
        functools.partial(pack_kernel, groups),
        out_shape=[rows] * groups + [pair] * groups,
        in_specs=[ANY] * 3,
        out_specs=[ANY] * (2 * groups),
        scratch_shapes=[pltpu.SemaphoreType.DMA((groups, 3))],
        compiler_params=params(4),
        cost_estimate=pl.CostEstimate(
            flops=0, bytes_accessed=4 * full * (parts * depth + 2 * tok), transcendentals=0
        ),
    )(weight, keys, values)
    return outs[:groups], outs[groups:]


def modulate_kernel(n_head, scale, shift, *refs):
    pieces, out, rows = refs[:n_head], refs[n_head], refs[n_head + 1]
    for hop, piece in enumerate(pieces):
        part = lax.rem(lax.axis_index("head") + (n_head - hop), n_head)
        rows[:, column(part, piece.shape[1])] = piece[...].astype(jnp.float32)
    states = rows[...]
    center = jnp.mean(states, axis=-1, keepdims=True)
    apart = states - center
    spread = jnp.mean(apart * apart, axis=-1, keepdims=True)
    normed = apart * lax.rsqrt(spread + 1e-06)
    out[...] = ((1.0 + scale[...]) * normed + shift[...]).astype(jnp.bfloat16)


def modulate(pieces, scale_mod, shift_mod):
    rows, _ = pieces[0].shape
    full = scale_mod.shape[0]
    return pl.pallas_call(
        functools.partial(modulate_kernel, len(pieces)),
        out_shape=jax.ShapeDtypeStruct((rows, full), jnp.bfloat16),
        in_specs=[VMEM] * (2 + len(pieces)),
        out_specs=VMEM,
        scratch_shapes=[pltpu.VMEM((rows, full), jnp.float32)],
        compiler_params=params(12),
        cost_estimate=pl.CostEstimate(
            flops=10 * rows * full, bytes_accessed=4 * rows * full, transcendentals=rows
        ),
    )(scale_mod.reshape(1, full), shift_mod.reshape(1, full), *pieces)


def project_kernel(groups, rest, n_mod, stacks, q_gain, k_gain, *refs):
    mods, arrays = refs[:n_mod], refs[n_mod : n_mod + len(stacks)]
    out, table = refs[n_mod + len(stacks) :]
    depth = arrays[0].shape[2]
    for array, keys in zip(arrays, stacks):
        for at, (step, bits) in enumerate(keys):
            patch = group_at(-step, groups) * rest + (lax.axis_index("rest") ^ bits)
            table[:, pl.ds(pl.multiple_of(patch * depth, 16), depth), :] = array[at]
    rows = jnp.concatenate([mod[...] for mod in mods], axis=0)
    size = q_gain.shape[1]
    for part in range(3):
        raw = jnp.dot(rows, table[part], preferred_element_type=jnp.float32)
        if part == 2:
            out[part] = raw.astype(jnp.bfloat16)
            continue
        gain = (q_gain, k_gain)[part][...]
        for head in range(raw.shape[1] // size):
            one = raw[:, head * size : (head + 1) * size]
            power = jnp.mean(one * one, axis=-1, keepdims=True)
            scaled = one * lax.rsqrt(power + 1e-06) * gain
            out[part, :, head * size : (head + 1) * size] = scaled.astype(jnp.bfloat16)


def project(mods, arrays, stacks, groups, rest, query_gain, key_gain):
    rows, full = mods[0].shape[0] * len(mods), mods[0].shape[1]
    width = arrays[0].shape[3]
    size = query_gain.shape[0]
    return pl.pallas_call(
        functools.partial(project_kernel, groups, rest, len(mods), stacks),
        out_shape=jax.ShapeDtypeStruct((3, rows, width), jnp.bfloat16),
        in_specs=[VMEM] * (2 + len(mods) + len(arrays)),
        out_specs=VMEM,
        scratch_shapes=[pltpu.VMEM((3, full, width), jnp.bfloat16)],
        compiler_params=params(16),
        cost_estimate=pl.CostEstimate(
            flops=6 * rows * full * width,
            bytes_accessed=2 * rows * full + 6 * full * width,
            transcendentals=0,
        ),
    )(query_gain.reshape(1, size), key_gain.reshape(1, size), *mods, *arrays)


def attend_kernel(groups, size, stacks, qkv, text_k, text_v, *refs):
    arrays, refs = refs[: len(stacks)], refs[len(stacks) :]
    outs, scores, weights = refs[:groups], refs[groups : groups + 2], refs[groups + 2 :]
    tok, width = outs[0].shape
    text, total = text_k.shape[0], scores[0].shape[1]
    heads, many = width // size, scores[0].shape[0]
    factor = size ** (-0.5)
    mine = lax.axis_index("group")
    slots = [key for keys in stacks for key in keys]
    windows = {}
    for index, (step, bits) in enumerate(slots):
        if bits == 0:
            windows[step] = slice(text + index * tok, text + (index + 1) * tok)

    def listed(cached, which, head):
        cols = slice(head * size, (head + 1) * size)
        rows = [cached[:, column(mine * heads + head, size)]]
        for array, keys in zip(arrays, stacks):
            rows += [array[at, which, :, cols] for at in range(len(keys))]
        return jnp.concatenate(rows, axis=0)

    def spot(index):
        head, begin = index % heads, index // heads * many
        blocks = range(begin // tok, (begin + many) // tok)
        return head, slice(head * size, (head + 1) * size), begin, blocks

    def multiply(index):
        head, cols, begin, blocks = spot(index)
        held = scores[index % 2]
        held[...] = lax.dot_general(
            qkv[0, begin : begin + many, cols],
            listed(text_k, 0, head),
            ACROSS,
            preferred_element_type=jnp.float32,
        )
        for block in blocks:
            rows = slice(block * tok, (block + 1) * tok)
            held[block * tok - begin : (block + 1) * tok - begin, windows[block]] = lax.dot_general(
                qkv[0, rows, cols], qkv[1, rows, cols], ACROSS, preferred_element_type=jnp.float32
            )

    count = groups * tok // many * heads
    multiply(0)
    for index in range(count):
        if index + 1 < count:
            multiply(index + 1)
        head, cols, begin, blocks = spot(index)
        held, soft = scores[index % 2], weights[index % 2]
        for block in blocks:
            here = slice(block * tok - begin, (block + 1) * tok - begin)
            most = held[here, :size]
            for at in range(size, total, size):
                most = jnp.maximum(most, held[here, at : at + size])
            peak = jnp.max(most, axis=-1, keepdims=True)
            summed = jnp.zeros((tok, size), jnp.float32)
            for at in range(0, total, size):
                exps = jnp.exp((held[here, at : at + size] - peak) * factor)
                summed += exps
                if windows[block].start == at:
                    fresh = exps.astype(jnp.bfloat16)
                    soft[here, at : at + size] = jnp.zeros((tok, size), jnp.bfloat16)
                else:
                    soft[here, at : at + size] = exps.astype(jnp.bfloat16)
            whole = jnp.sum(summed, axis=-1, keepdims=True)
            own = qkv[2, block * tok : (block + 1) * tok, cols]
            mixed = jnp.dot(fresh, own, preferred_element_type=jnp.float32)
            mixed += jnp.dot(
                soft[here, :], listed(text_v, 1, head), preferred_element_type=jnp.float32
            )
            outs[block][:, cols] = (mixed / whole).astype(jnp.bfloat16)


def attend(qkv, text_keys, text_values, arrays, stacks, groups, size):
    _, rows, width = qkv.shape
    tok = rows // groups
    total = text_keys.shape[0] + tok * sum(len(keys) for keys in stacks)
    many = tok * (2 if groups % 2 == 0 else 1)
    return pl.pallas_call(
        functools.partial(attend_kernel, groups, size, stacks),
        out_shape=[jax.ShapeDtypeStruct((tok, width), jnp.bfloat16)] * groups,
        in_specs=[VMEM] * (3 + len(arrays)),
        out_specs=[VMEM] * groups,
        scratch_shapes=[
            pltpu.VMEM((many, total), jnp.float32),
            pltpu.VMEM((many, total), jnp.float32),
            pltpu.VMEM((many, total), jnp.bfloat16),
            pltpu.VMEM((many, total), jnp.bfloat16),
        ],
        compiler_params=params(24),
        cost_estimate=pl.CostEstimate(
            flops=4 * rows * width * total,
            bytes_accessed=4 * total * width,
            transcendentals=rows * (width // size) * total,
        ),
    )(qkv, text_keys, text_values, *arrays)


def combine_kernel(hop, n_head, weight, *refs):
    pieces, out, rows = refs[:-2], refs[-2], refs[-1]
    wide = pieces[0].shape[1]
    for step, piece in enumerate(pieces):
        rows[:, column(group_at(step, len(pieces)), wide)] = piece[...]
    side = lax.rem(lax.axis_index("head") + hop, n_head)
    table = weight[:, column(side, out.shape[1])]
    out[...] = jnp.dot(rows[...], table, preferred_element_type=jnp.float32).astype(out.dtype)


def combine(pieces, hop, n_head, weight, share, kind):
    tok = pieces[0].shape[0]
    depth = weight.shape[0]
    return pl.pallas_call(
        functools.partial(combine_kernel, hop, n_head),
        out_shape=jax.ShapeDtypeStruct((tok, share), kind),
        in_specs=[VMEM] * (1 + len(pieces)),
        out_specs=VMEM,
        scratch_shapes=[pltpu.VMEM((tok, depth), jnp.bfloat16)],
        compiler_params=params(6),
        cost_estimate=pl.CostEstimate(
            flops=2 * tok * depth * share, bytes_accessed=2 * depth * share, transcendentals=0
        ),
    )(weight, *pieces)


def after(array, *others):
    return lax.optimization_barrier((array, *others))[0] if others else array


def per_device(
    groups,
    rest,
    n_head,
    hidden_states,
    shift_mod,
    scale_mod,
    gate_mod,
    qkv_weight,
    query_gain,
    key_gain,
    text_keys,
    text_values,
    stale_keys,
    stale_values,
    out_weight,
):
    tok, share = hidden_states.shape
    size = query_gain.shape[0]

    def turn(array, step):
        pairs = [(i, gray((gray(i) + step) % groups)) for i in range(groups)]
        return lax.ppermute(array, "group", pairs)

    def swap(array, bit):
        return lax.ppermute(array, "rest", [(i, i ^ bit) for i in range(rest)])

    def across(array, hop):
        return lax.ppermute(array, "head", [(i, (i + hop) % n_head) for i in range(n_head)])

    def finish(found, last, ready):
        bit = rest // 2
        while bit > 1:
            for (step, bits), piece in list(found.items()):
                if last is not None:
                    piece = after(piece, last)
                found[step, bits | bit] = last = swap(piece, bit)
            bit //= 2
        names = list(found)
        stacks = [[name] for name in names]
        arrays = [found[name][None] for name in names]
        if bit:
            early = [name for name in names[:-1] if name[0] < groups // 2]
            late = [name for name in names[:-1] if name[0] >= groups // 2]
            for cut in (early, late, names[-1:]):
                if not cut:
                    continue
                pieces = [found[name] for name in cut]
                stack = jnp.stack(pieces) if len(cut) > 1 else pieces[0][None]
                if cut[-1] == names[-1]:
                    stack = after(stack, *ready)
                arrays.append(swap(stack, bit))
                stacks.append([(step, bits | bit) for step, bits in cut])
        return arrays, stacks, last

    moving, last = hidden_states, None
    mods, hops, sides = [], [], []
    for step in range(groups):
        if step:
            moving = turn(after(moving, *sides[: step - 1]), 1)
            hops.append(moving)
        slices = [moving]
        for hop in range(1, n_head):
            last = across(moving if last is None else after(moving, last), hop)
            slices.append(last)
            sides.append(last)
        mods.append(modulate(slices, scale_mod, shift_mod))

    packed, pairs = pack(jnp.transpose(qkv_weight, (1, 0, 2)), stale_keys, stale_values, groups)
    rows, cached = {(0, 0): packed[0]}, {(0, 0): pairs[0]}
    before = []
    for step in range(1, groups):
        before = before + hops[step - 1 : step]
        rows[step, 0] = turn(after(packed[step], *before), step)
        before = [rows[step, 0]]
    for step in range(1, groups):
        before = [rows[min(step + 1, groups - 1), 0]] + (mods[:step] if step > 1 else [])
        cached[step, 0] = turn(after(pairs[step], *before), step)
    arrays, stacks, last = finish(rows, None, mods[-1:])
    qkv = project(mods, arrays, stacks, groups, rest, query_gain, key_gain)
    arrays, stacks, _ = finish(cached, last, [])
    attention = attend(qkv, text_keys, text_values, arrays, stacks, groups, size)
    pieces = [attention[0]] + [turn(attention[step], -step) for step in range(1, groups)]
    terms = []
    for hop in range(1, n_head):
        term = combine(pieces, hop, n_head, out_weight, share, jnp.bfloat16)
        terms.append(across(term, hop))
    summed = combine(pieces, 0, n_head, out_weight, share, jnp.float32)
    for term in terms:
        summed = summed + term.astype(jnp.float32)
    return (summed * gate_mod).astype(jnp.bfloat16)


def solution(mesh):
    n_patch, n_head = mesh.shape["patch"], mesh.shape["head"]

    def whole(*arrays):
        heads = arrays[4].shape[2] // n_head // arrays[5].shape[0]
        groups = math.gcd(math.gcd(4, heads), n_patch)
        rest = n_patch // groups
        cut = Mesh(mesh.devices.reshape(groups, rest, n_head), ("group", "rest", "head"))
        patch = ("group", "rest")
        placed = (
            P(patch, "head"),
            P(),
            P(),
            P("head"),
            P(patch, None, "head"),
            P(),
            P(),
            P(None, "head"),
            P(None, "head"),
            P(patch, "head"),
            P(patch, "head"),
            P("head", None),
        )
        return jax.shard_map(
            functools.partial(per_device, groups, rest, n_head),
            mesh=cut,
            in_specs=placed,
            out_specs=P(patch, "head"),
            check_vma=False,
        )(*arrays)

    return whole
```

```python
import functools
import math

import jax
import jax.numpy as jnp
from jax import lax
from jax.experimental import pallas as pl
from jax.experimental.pallas import tpu as pltpu
from jax.sharding import Mesh
from jax.sharding import PartitionSpec as P

ANY = pl.BlockSpec(memory_space=pl.ANY)
VMEM = pl.BlockSpec(memory_space=pltpu.VMEM)
MIB = 1024 * 1024
NO_COST = pl.CostEstimate(flops=0, bytes_accessed=0, transcendentals=0)
ACROSS = (((1,), (1,)), ((), ()))


def params(limit):
    return pltpu.CompilerParams(vmem_limit_bytes=limit * MIB)


def column(index, width):
    return pl.ds(pl.multiple_of(index * width, 128), width)


def gray(place):
    return place ^ (place >> 1)


def group_at(step, groups):
    return gray(lax.rem(gray(lax.axis_index("group")) + (step + groups), groups))


def pack_kernel(groups, weight, keys, values, *refs):
    outs, sems = refs[:-1], refs[-1]
    started = []
    for step in range(groups):
        rows, pair = outs[step], outs[groups + step]
        cols = column(group_at(step, groups), rows.shape[2])
        copies = [(weight.at[:, :, cols], rows)]
        copies += [(keys.at[:, cols], pair.at[0]), (values.at[:, cols], pair.at[1])]
        for index, (source, target) in enumerate(copies):
            copy = pltpu.make_async_copy(source, target, sems.at[step, index])
            copy.start()
            started.append(copy)
    for copy in started:
        copy.wait()


def pack(weight, keys, values, groups):
    parts, depth, full = weight.shape
    tok, width = keys.shape[0], full // groups
    rows = jax.ShapeDtypeStruct((parts, depth, width), jnp.bfloat16)
    pair = jax.ShapeDtypeStruct((2, tok, width), jnp.bfloat16)
    outs = pl.pallas_call(
        functools.partial(pack_kernel, groups),
        out_shape=[rows] * groups + [pair] * groups,
        in_specs=[ANY] * 3,
        out_specs=[ANY] * (2 * groups),
        scratch_shapes=[pltpu.SemaphoreType.DMA((groups, 3))],
        compiler_params=params(4),
        cost_estimate=NO_COST,
    )(weight, keys, values)
    return outs[:groups], outs[groups:]


def stack_kernel(*refs):
    pieces, out, sems = refs[:-2], refs[-2], refs[-1]
    started = []
    for index, piece in enumerate(pieces):
        started.append(pltpu.make_async_copy(piece, out.at[index], sems.at[index]))
        started[-1].start()
    for copy in started:
        copy.wait()


def stack(pieces):
    shape = (len(pieces), *pieces[0].shape)
    return pl.pallas_call(
        stack_kernel,
        out_shape=jax.ShapeDtypeStruct(shape, pieces[0].dtype),
        in_specs=[ANY] * len(pieces),
        out_specs=ANY,
        scratch_shapes=[pltpu.SemaphoreType.DMA((len(pieces),))],
        compiler_params=params(4),
        cost_estimate=NO_COST,
    )(*pieces)


def modulate_kernel(n_head, scale, shift, *refs):
    pieces, out, rows = refs[:n_head], refs[n_head], refs[n_head + 1]
    for hop, piece in enumerate(pieces):
        part = lax.rem(lax.axis_index("head") + (n_head - hop), n_head)
        rows[:, column(part, piece.shape[1])] = piece[...].astype(jnp.float32)
    states = rows[...]
    center = jnp.mean(states, axis=-1, keepdims=True)
    apart = states - center
    spread = jnp.mean(apart * apart, axis=-1, keepdims=True)
    normed = apart * lax.rsqrt(spread + 1e-06)
    out[...] = ((1.0 + scale[...]) * normed + shift[...]).astype(jnp.bfloat16)


def modulate(pieces, scale_mod, shift_mod):
    rows, _ = pieces[0].shape
    full = scale_mod.shape[0]
    return pl.pallas_call(
        functools.partial(modulate_kernel, len(pieces)),
        out_shape=jax.ShapeDtypeStruct((rows, full), jnp.bfloat16),
        in_specs=[VMEM] * (2 + len(pieces)),
        out_specs=VMEM,
        scratch_shapes=[pltpu.VMEM((rows, full), jnp.float32)],
        compiler_params=params(12),
        cost_estimate=NO_COST,
    )(scale_mod.reshape(1, full), shift_mod.reshape(1, full), *pieces)


def project_kernel(groups, rest, n_mod, stacks, q_gain, k_gain, *refs):
    mods, arrays = refs[:n_mod], refs[n_mod : n_mod + len(stacks)]
    out, table = refs[n_mod + len(stacks) :]
    depth = arrays[0].shape[2]
    for array, keys in zip(arrays, stacks):
        for at, (step, bits) in enumerate(keys):
            patch = group_at(-step, groups) * rest + (lax.axis_index("rest") ^ bits)
            table[:, pl.ds(pl.multiple_of(patch * depth, 16), depth), :] = array[at]
    rows = jnp.concatenate([mod[...] for mod in mods], axis=0)
    size = q_gain.shape[1]
    for part in range(3):
        raw = jnp.dot(rows, table[part], preferred_element_type=jnp.float32)
        if part == 2:
            out[part] = raw.astype(jnp.bfloat16)
            continue
        gain = (q_gain, k_gain)[part][...]
        for head in range(raw.shape[1] // size):
            one = raw[:, head * size : (head + 1) * size]
            power = jnp.mean(one * one, axis=-1, keepdims=True)
            scaled = one * lax.rsqrt(power + 1e-06) * gain
            out[part, :, head * size : (head + 1) * size] = scaled.astype(jnp.bfloat16)


def project(mods, arrays, stacks, groups, rest, query_gain, key_gain):
    rows, full = mods[0].shape[0] * len(mods), mods[0].shape[1]
    width = arrays[0].shape[3]
    size = query_gain.shape[0]
    return pl.pallas_call(
        functools.partial(project_kernel, groups, rest, len(mods), stacks),
        out_shape=jax.ShapeDtypeStruct((3, rows, width), jnp.bfloat16),
        in_specs=[VMEM] * (2 + len(mods) + len(arrays)),
        out_specs=VMEM,
        scratch_shapes=[pltpu.VMEM((3, full, width), jnp.bfloat16)],
        compiler_params=params(16),
        cost_estimate=NO_COST,
    )(query_gain.reshape(1, size), key_gain.reshape(1, size), *mods, *arrays)


def attend_kernel(groups, size, stacks, qkv, text_k, text_v, *refs):
    arrays, refs = refs[: len(stacks)], refs[len(stacks) :]
    outs, scores, weights = refs[:groups], refs[groups : groups + 2], refs[groups + 2 :]
    tok, width = outs[0].shape
    text, total = text_k.shape[0], scores[0].shape[1]
    heads, many = width // size, scores[0].shape[0]
    factor = size ** (-0.5)
    mine = lax.axis_index("group")
    slots = [key for keys in stacks for key in keys]
    windows = {}
    for index, (step, bits) in enumerate(slots):
        if bits == 0:
            windows[step] = slice(text + index * tok, text + (index + 1) * tok)

    def listed(cached, which, head):
        cols = slice(head * size, (head + 1) * size)
        rows = [cached[:, column(mine * heads + head, size)]]
        for array, keys in zip(arrays, stacks):
            rows += [array[at, which, :, cols] for at in range(len(keys))]
        return jnp.concatenate(rows, axis=0)

    def spot(index):
        head, begin = index % heads, index // heads * many
        blocks = range(begin // tok, (begin + many) // tok)
        return head, slice(head * size, (head + 1) * size), begin, blocks

    def multiply(index):
        head, cols, begin, blocks = spot(index)
        held = scores[index % 2]
        held[...] = lax.dot_general(
            qkv[0, begin : begin + many, cols],
            listed(text_k, 0, head),
            ACROSS,
            preferred_element_type=jnp.float32,
        )
        for block in blocks:
            rows = slice(block * tok, (block + 1) * tok)
            held[block * tok - begin : (block + 1) * tok - begin, windows[block]] = lax.dot_general(
                qkv[0, rows, cols], qkv[1, rows, cols], ACROSS, preferred_element_type=jnp.float32
            )

    count = groups * tok // many * heads
    multiply(0)
    for index in range(count):
        if index + 1 < count:
            multiply(index + 1)
        head, cols, begin, blocks = spot(index)
        held, soft = scores[index % 2], weights[index % 2]
        for block in blocks:
            here = slice(block * tok - begin, (block + 1) * tok - begin)
            most = held[here, :size]
            for at in range(size, total, size):
                most = jnp.maximum(most, held[here, at : at + size])
            peak = jnp.max(most, axis=-1, keepdims=True)
            summed = jnp.zeros((tok, size), jnp.float32)
            for at in range(0, total, size):
                exps = jnp.exp((held[here, at : at + size] - peak) * factor)
                summed += exps
                if windows[block].start == at:
                    fresh = exps.astype(jnp.bfloat16)
                    soft[here, at : at + size] = jnp.zeros((tok, size), jnp.bfloat16)
                else:
                    soft[here, at : at + size] = exps.astype(jnp.bfloat16)
            whole = jnp.sum(summed, axis=-1, keepdims=True)
            own = qkv[2, block * tok : (block + 1) * tok, cols]
            mixed = jnp.dot(fresh, own, preferred_element_type=jnp.float32)
            mixed += jnp.dot(
                soft[here, :], listed(text_v, 1, head), preferred_element_type=jnp.float32
            )
            outs[block][:, cols] = (mixed / whole).astype(jnp.bfloat16)


def attend(qkv, text_keys, text_values, arrays, stacks, groups, size):
    _, rows, width = qkv.shape
    tok = rows // groups
    total = text_keys.shape[0] + tok * sum(len(keys) for keys in stacks)
    many = tok * (2 if groups % 2 == 0 else 1)
    return pl.pallas_call(
        functools.partial(attend_kernel, groups, size, stacks),
        out_shape=[jax.ShapeDtypeStruct((tok, width), jnp.bfloat16)] * groups,
        in_specs=[VMEM] * (3 + len(arrays)),
        out_specs=[VMEM] * groups,
        scratch_shapes=[
            pltpu.VMEM((many, total), jnp.float32),
            pltpu.VMEM((many, total), jnp.float32),
            pltpu.VMEM((many, total), jnp.bfloat16),
            pltpu.VMEM((many, total), jnp.bfloat16),
        ],
        compiler_params=params(24),
        cost_estimate=NO_COST,
    )(qkv, text_keys, text_values, *arrays)


def combine_kernel(hop, n_head, weight, *refs):
    pieces, out, rows = refs[:-2], refs[-2], refs[-1]
    wide = pieces[0].shape[1]
    for step, piece in enumerate(pieces):
        rows[:, column(group_at(step, len(pieces)), wide)] = piece[...]
    side = lax.rem(lax.axis_index("head") + hop, n_head)
    table = weight[:, column(side, out.shape[1])]
    out[...] = jnp.dot(rows[...], table, preferred_element_type=jnp.float32).astype(out.dtype)


def combine(pieces, hop, n_head, weight, share, kind):
    tok = pieces[0].shape[0]
    depth = weight.shape[0]
    return pl.pallas_call(
        functools.partial(combine_kernel, hop, n_head),
        out_shape=jax.ShapeDtypeStruct((tok, share), kind),
        in_specs=[VMEM] * (1 + len(pieces)),
        out_specs=VMEM,
        scratch_shapes=[pltpu.VMEM((tok, depth), jnp.bfloat16)],
        compiler_params=params(6),
        cost_estimate=NO_COST,
    )(weight, *pieces)


def after(array, *others):
    return lax.optimization_barrier((array, *others))[0] if others else array


def per_device(
    groups,
    rest,
    n_head,
    hidden_states,
    shift_mod,
    scale_mod,
    gate_mod,
    qkv_weight,
    query_gain,
    key_gain,
    text_keys,
    text_values,
    stale_keys,
    stale_values,
    out_weight,
):
    tok, share = hidden_states.shape
    size = query_gain.shape[0]

    def turn(array, step):
        pairs = [(i, gray((gray(i) + step) % groups)) for i in range(groups)]
        return lax.ppermute(array, "group", pairs)

    def swap(array, bit):
        return lax.ppermute(array, "rest", [(i, i ^ bit) for i in range(rest)])

    def across(array, hop):
        return lax.ppermute(array, "head", [(i, (i + hop) % n_head) for i in range(n_head)])

    def spread(found, step, *ready):
        bit = rest // 2
        while bit > 1:
            for (mark, bits), piece in list(found.items()):
                if mark == step:
                    found[step, bits | bit] = swap(after(piece, *ready), bit)
            bit //= 2
        return found[step, max(bits for mark, bits in found if mark == step)]

    def finish(found, last_step, early_waits, late_waits):
        names = list(found)
        stacks = [[name] for name in names]
        arrays = [found[name][None] for name in names]
        if rest % 2 == 0:
            early = [name for name in names if name[0] != last_step]
            late = [name for name in names if name[0] == last_step]
            for part, waits in ((early, early_waits), (late, late_waits)):
                if not part:
                    continue
                pieces = [found[name] for name in part]
                pieces[0] = after(pieces[0], *waits)
                joined = stack(pieces) if len(part) > 1 else pieces[0][None]
                arrays.append(swap(joined, 1))
                stacks.append([(step, bits | 1) for step, bits in part])
        return arrays, stacks

    packed, pairs = pack(jnp.transpose(qkv_weight, (1, 0, 2)), stale_keys, stale_values, groups)
    found, cached = {(0, 0): packed[0]}, {(0, 0): pairs[0]}
    mods, hops, crossed, swapped = [], [], [], []

    def cross(piece, *ready):
        slices = [piece]
        for hop in range(1, n_head):
            slices.append(across(after(piece, *ready), hop))
            crossed.append(slices[-1])
        mods.append(modulate(slices, scale_mod, shift_mod))

    cross(hidden_states)
    swapped.append(spread(found, 0))
    order = [1, *range(groups - 1, 1, -1)][: groups - 1]
    for index, step in enumerate(order):
        ready = [found[order[0], 0]] if index > 1 else crossed[:1]
        hops.append(turn(after(hops[-1], *ready) if hops else hidden_states, 1))
        ready = [found[order[0], 0]] if index > 1 else []
        found[step, 0] = turn(after(packed[step], *hops[:1], *crossed[:1], *ready), step)
        cross(hops[-1], *crossed[-1:], *packed[:1])
    for index, step in enumerate(order):
        ready = hops[1:2] if index == 0 else []
        ready += crossed[: (index + 2) * (n_head - 1)] if index < 2 else []
        swapped.append(spread(found, step, *swapped[-1:], *ready))
    for index, step in enumerate(order):
        ready = [found[order[min(1, groups - 2)], 0], *swapped[1:2]]
        ready += [] if index == 0 else hops[-1:]
        cached[step, 0] = turn(after(pairs[step], *ready), step)
    spread(cached, 0, *swapped[2:3])
    for step in order:
        spread(cached, step, *swapped[2:3])
    last_step = order[-1] if order else 0
    waits = [found[step, 0] for step in order] + [cached[step, 0] for step in order[:1]]
    waits += crossed[: 1 - n_head] + swapped[:-1] + hops[-1:]
    arrays, stacks = finish(found, last_step, waits, mods + [cached[last_step, 0]])
    qkv = project(mods, arrays, stacks, groups, rest, query_gain, key_gain)
    arrays, stacks = finish(cached, last_step, [], [])
    attention = attend(qkv, text_keys, text_values, arrays, stacks, groups, size)
    pieces = [attention[0]] + [turn(attention[step], -step) for step in range(1, groups)]
    terms = []
    for hop in range(1, n_head):
        term = combine(pieces, hop, n_head, out_weight, share, jnp.bfloat16)
        terms.append(across(term, hop))
    summed = combine(pieces, 0, n_head, out_weight, share, jnp.float32)
    for term in terms:
        summed = summed + term.astype(jnp.float32)
    return (summed * gate_mod).astype(jnp.bfloat16)


def solution(mesh):
    n_patch, n_head = mesh.shape["patch"], mesh.shape["head"]

    def whole(*arrays):
        heads = arrays[4].shape[2] // n_head // arrays[5].shape[0]
        groups = math.gcd(math.gcd(4, heads), n_patch)
        rest = n_patch // groups
        cut = Mesh(mesh.devices.reshape(groups, rest, n_head), ("group", "rest", "head"))
        patch = ("group", "rest")
        placed = (
            P(patch, "head"),
            P(),
            P(),
            P("head"),
            P(patch, None, "head"),
            P(),
            P(),
            P(None, "head"),
            P(None, "head"),
            P(patch, "head"),
            P(patch, "head"),
            P("head", None),
        )
        return jax.shard_map(
            functools.partial(per_device, groups, rest, n_head),
            mesh=cut,
            in_specs=placed,
            out_specs=P(patch, "head"),
            check_vma=False,
        )(*arrays)

    return whole
```

```python
import functools
import math

import jax
import jax.numpy as jnp
from jax import lax
from jax.experimental import pallas as pl
from jax.experimental.pallas import tpu as pltpu
from jax.sharding import Mesh
from jax.sharding import PartitionSpec as P

ANY = pl.BlockSpec(memory_space=pl.ANY)
VMEM = pl.BlockSpec(memory_space=pltpu.VMEM)
MIB = 1024 * 1024
NO_COST = pl.CostEstimate(flops=0, bytes_accessed=0, transcendentals=0)
ACROSS = (((1,), (1,)), ((), ()))


def params(limit):
    return pltpu.CompilerParams(vmem_limit_bytes=limit * MIB)


def column(index, width):
    return pl.ds(pl.multiple_of(index * width, 128), width)


def gray(place):
    return place ^ (place >> 1)


def group_at(step, groups):
    return gray(lax.rem(gray(lax.axis_index("group")) + (step + groups), groups))


def pack_kernel(groups, weight, keys, values, *refs):
    outs, sems = refs[:-1], refs[-1]
    started = []
    for step in range(groups):
        rows, pair = outs[step], outs[groups + step]
        cols = column(group_at(step, groups), rows.shape[2])
        copies = [(weight.at[:, :, cols], rows)]
        copies += [(keys.at[:, cols], pair.at[0]), (values.at[:, cols], pair.at[1])]
        for index, (source, target) in enumerate(copies):
            copy = pltpu.make_async_copy(source, target, sems.at[step, index])
            copy.start()
            started.append(copy)
    for copy in started:
        copy.wait()


def pack(weight, keys, values, groups):
    parts, depth, full = weight.shape
    tok, width = keys.shape[0], full // groups
    rows = jax.ShapeDtypeStruct((parts, depth, width), jnp.bfloat16)
    pair = jax.ShapeDtypeStruct((2, tok, width), jnp.bfloat16)
    outs = pl.pallas_call(
        functools.partial(pack_kernel, groups),
        out_shape=[rows] * groups + [pair] * groups,
        in_specs=[ANY] * 3,
        out_specs=[ANY] * (2 * groups),
        scratch_shapes=[pltpu.SemaphoreType.DMA((groups, 3))],
        compiler_params=params(4),
        cost_estimate=NO_COST,
    )(weight, keys, values)
    return outs[:groups], outs[groups:]


def stack_kernel(*refs):
    pieces, out, sems = refs[:-2], refs[-2], refs[-1]
    started = []
    for index, piece in enumerate(pieces):
        started.append(pltpu.make_async_copy(piece, out.at[index], sems.at[index]))
        started[-1].start()
    for copy in started:
        copy.wait()


def stack(pieces):
    shape = (len(pieces), *pieces[0].shape)
    return pl.pallas_call(
        stack_kernel,
        out_shape=jax.ShapeDtypeStruct(shape, pieces[0].dtype),
        in_specs=[ANY] * len(pieces),
        out_specs=ANY,
        scratch_shapes=[pltpu.SemaphoreType.DMA((len(pieces),))],
        compiler_params=params(4),
        cost_estimate=NO_COST,
    )(*pieces)


def modulate_kernel(n_head, scale, shift, *refs):
    pieces, out, rows = refs[:n_head], refs[n_head], refs[n_head + 1]
    for hop, piece in enumerate(pieces):
        part = lax.rem(lax.axis_index("head") + (n_head - hop), n_head)
        rows[:, column(part, piece.shape[1])] = piece[...].astype(jnp.float32)
    states = rows[...]
    center = jnp.mean(states, axis=-1, keepdims=True)
    apart = states - center
    spread = jnp.mean(apart * apart, axis=-1, keepdims=True)
    normed = apart * lax.rsqrt(spread + 1e-06)
    out[...] = ((1.0 + scale[...]) * normed + shift[...]).astype(jnp.bfloat16)


def modulate(pieces, scale_mod, shift_mod):
    rows, _ = pieces[0].shape
    full = scale_mod.shape[0]
    return pl.pallas_call(
        functools.partial(modulate_kernel, len(pieces)),
        out_shape=jax.ShapeDtypeStruct((rows, full), jnp.bfloat16),
        in_specs=[VMEM] * (2 + len(pieces)),
        out_specs=VMEM,
        scratch_shapes=[pltpu.VMEM((rows, full), jnp.float32)],
        compiler_params=params(12),
        cost_estimate=NO_COST,
    )(scale_mod.reshape(1, full), shift_mod.reshape(1, full), *pieces)


def project_kernel(groups, rest, n_mod, stacks, q_gain, k_gain, *refs):
    mods, arrays = refs[:n_mod], refs[n_mod : n_mod + len(stacks)]
    out, table = refs[n_mod + len(stacks) :]
    depth = arrays[0].shape[2]
    for array, keys in zip(arrays, stacks):
        for at, (step, bits) in enumerate(keys):
            patch = group_at(-step, groups) * rest + (lax.axis_index("rest") ^ bits)
            table[:, pl.ds(pl.multiple_of(patch * depth, 16), depth), :] = array[at]
    rows = jnp.concatenate([mod[...] for mod in mods], axis=0)
    size = q_gain.shape[1]
    for part in range(3):
        raw = jnp.dot(rows, table[part], preferred_element_type=jnp.float32)
        if part == 2:
            out[part] = raw.astype(jnp.bfloat16)
            continue
        gain = (q_gain, k_gain)[part][...]
        for head in range(raw.shape[1] // size):
            one = raw[:, head * size : (head + 1) * size]
            power = jnp.mean(one * one, axis=-1, keepdims=True)
            scaled = one * lax.rsqrt(power + 1e-06) * gain
            out[part, :, head * size : (head + 1) * size] = scaled.astype(jnp.bfloat16)


def project(mods, arrays, stacks, groups, rest, query_gain, key_gain):
    rows, full = mods[0].shape[0] * len(mods), mods[0].shape[1]
    width = arrays[0].shape[3]
    size = query_gain.shape[0]
    return pl.pallas_call(
        functools.partial(project_kernel, groups, rest, len(mods), stacks),
        out_shape=jax.ShapeDtypeStruct((3, rows, width), jnp.bfloat16),
        in_specs=[VMEM] * (2 + len(mods) + len(arrays)),
        out_specs=VMEM,
        scratch_shapes=[pltpu.VMEM((3, full, width), jnp.bfloat16)],
        compiler_params=params(16),
        cost_estimate=NO_COST,
    )(query_gain.reshape(1, size), key_gain.reshape(1, size), *mods, *arrays)


def attend_kernel(groups, size, stacks, qkv, text_k, text_v, *refs):
    arrays, refs = refs[: len(stacks)], refs[len(stacks) :]
    outs, scores, weights = refs[:groups], refs[groups : groups + 2], refs[groups + 2 :]
    tok, width = outs[0].shape
    text, total = text_k.shape[0], scores[0].shape[1]
    heads, many = width // size, scores[0].shape[0]
    factor = size ** (-0.5)
    mine = lax.axis_index("group")
    slots = [key for keys in stacks for key in keys]
    windows = {}
    for index, (step, bits) in enumerate(slots):
        if bits == 0:
            windows[step] = slice(text + index * tok, text + (index + 1) * tok)

    def listed(cached, which, head):
        cols = slice(head * size, (head + 1) * size)
        rows = [cached[:, column(mine * heads + head, size)]]
        for array, keys in zip(arrays, stacks):
            rows += [array[at, which, :, cols] for at in range(len(keys))]
        return jnp.concatenate(rows, axis=0)

    def spot(index):
        head, begin = index % heads, index // heads * many
        blocks = range(begin // tok, (begin + many) // tok)
        return head, slice(head * size, (head + 1) * size), begin, blocks

    def multiply(index):
        head, cols, begin, blocks = spot(index)
        held = scores[index % 2]
        held[...] = lax.dot_general(
            qkv[0, begin : begin + many, cols],
            listed(text_k, 0, head),
            ACROSS,
            preferred_element_type=jnp.float32,
        )
        for block in blocks:
            rows = slice(block * tok, (block + 1) * tok)
            held[block * tok - begin : (block + 1) * tok - begin, windows[block]] = lax.dot_general(
                qkv[0, rows, cols], qkv[1, rows, cols], ACROSS, preferred_element_type=jnp.float32
            )

    count = groups * tok // many * heads
    multiply(0)
    for index in range(count):
        if index + 1 < count:
            multiply(index + 1)
        head, cols, begin, blocks = spot(index)
        held, soft = scores[index % 2], weights[index % 2]
        for block in blocks:
            here = slice(block * tok - begin, (block + 1) * tok - begin)
            most = held[here, :size]
            for at in range(size, total, size):
                most = jnp.maximum(most, held[here, at : at + size])
            peak = jnp.max(most, axis=-1, keepdims=True)
            summed = jnp.zeros((tok, size), jnp.float32)
            for at in range(0, total, size):
                exps = jnp.exp((held[here, at : at + size] - peak) * factor)
                summed += exps
                if windows[block].start == at:
                    fresh = exps.astype(jnp.bfloat16)
                    soft[here, at : at + size] = jnp.zeros((tok, size), jnp.bfloat16)
                else:
                    soft[here, at : at + size] = exps.astype(jnp.bfloat16)
            whole = jnp.sum(summed, axis=-1, keepdims=True)
            own = qkv[2, block * tok : (block + 1) * tok, cols]
            mixed = jnp.dot(fresh, own, preferred_element_type=jnp.float32)
            mixed += jnp.dot(
                soft[here, :], listed(text_v, 1, head), preferred_element_type=jnp.float32
            )
            outs[block][:, cols] = (mixed / whole).astype(jnp.bfloat16)


def attend(qkv, text_keys, text_values, arrays, stacks, groups, size):
    _, rows, width = qkv.shape
    tok = rows // groups
    total = text_keys.shape[0] + tok * sum(len(keys) for keys in stacks)
    many = tok * (2 if groups % 2 == 0 else 1)
    return pl.pallas_call(
        functools.partial(attend_kernel, groups, size, stacks),
        out_shape=[jax.ShapeDtypeStruct((tok, width), jnp.bfloat16)] * groups,
        in_specs=[VMEM] * (3 + len(arrays)),
        out_specs=[VMEM] * groups,
        scratch_shapes=[
            pltpu.VMEM((many, total), jnp.float32),
            pltpu.VMEM((many, total), jnp.float32),
            pltpu.VMEM((many, total), jnp.bfloat16),
            pltpu.VMEM((many, total), jnp.bfloat16),
        ],
        compiler_params=params(24),
        cost_estimate=NO_COST,
    )(qkv, text_keys, text_values, *arrays)


def combine_kernel(hop, n_head, weight, *refs):
    pieces, out, rows = refs[:-2], refs[-2], refs[-1]
    wide = pieces[0].shape[1]
    for step, piece in enumerate(pieces):
        rows[:, column(group_at(step, len(pieces)), wide)] = piece[...]
    side = lax.rem(lax.axis_index("head") + hop, n_head)
    table = weight[:, column(side, out.shape[1])]
    out[...] = jnp.dot(rows[...], table, preferred_element_type=jnp.float32).astype(out.dtype)


def combine(pieces, hop, n_head, weight, share, kind):
    tok = pieces[0].shape[0]
    depth = weight.shape[0]
    return pl.pallas_call(
        functools.partial(combine_kernel, hop, n_head),
        out_shape=jax.ShapeDtypeStruct((tok, share), kind),
        in_specs=[VMEM] * (1 + len(pieces)),
        out_specs=VMEM,
        scratch_shapes=[pltpu.VMEM((tok, depth), jnp.bfloat16)],
        compiler_params=params(6),
        cost_estimate=NO_COST,
    )(weight, *pieces)


def after(array, *others):
    return lax.optimization_barrier((array, *others))[0] if others else array


def per_device(
    groups,
    rest,
    n_head,
    hidden_states,
    shift_mod,
    scale_mod,
    gate_mod,
    qkv_weight,
    query_gain,
    key_gain,
    text_keys,
    text_values,
    stale_keys,
    stale_values,
    out_weight,
):
    tok, share = hidden_states.shape
    size = query_gain.shape[0]

    def turn(array, step):
        pairs = [(i, gray((gray(i) + step) % groups)) for i in range(groups)]
        return lax.ppermute(array, "group", pairs)

    def swap(array, bit):
        return lax.ppermute(array, "rest", [(i, i ^ bit) for i in range(rest)])

    def across(array, hop):
        return lax.ppermute(array, "head", [(i, (i + hop) % n_head) for i in range(n_head)])

    def spread(found, step, *ready):
        bit = rest // 2
        while bit > 1:
            for (mark, bits), piece in list(found.items()):
                if mark == step:
                    found[step, bits | bit] = swap(after(piece, *ready), bit)
            bit //= 2
        return found[step, max(bits for mark, bits in found if mark == step)]

    def finish(found, last_step, early_waits, late_waits):
        names = list(found)
        stacks = [[name] for name in names]
        arrays = [found[name][None] for name in names]
        if rest % 2 == 0:
            early = [name for name in names if name[0] != last_step]
            late = [name for name in names if name[0] == last_step]
            for part, waits in ((early, early_waits), (late, late_waits)):
                if not part:
                    continue
                pieces = [found[name] for name in part]
                pieces[0] = after(pieces[0], *waits)
                joined = stack(pieces) if len(part) > 1 else pieces[0][None]
                arrays.append(swap(joined, 1))
                stacks.append([(step, bits | 1) for step, bits in part])
        return arrays, stacks

    packed, pairs = pack(jnp.transpose(qkv_weight, (1, 0, 2)), stale_keys, stale_values, groups)
    found, cached = {(0, 0): packed[0]}, {(0, 0): pairs[0]}
    mods, hops, crossed, swapped = [], [], [], []

    def cross(piece, *ready):
        slices = [piece]
        for hop in range(1, n_head):
            slices.append(across(after(piece, *ready), hop))
            crossed.append(slices[-1])
        mods.append(modulate(slices, scale_mod, shift_mod))

    cross(hidden_states)
    swapped.append(spread(found, 0))
    ahead = []
    order = [1, *range(groups - 1, 1, -1)][: groups - 1]
    for index, step in enumerate(order):
        ready = [found[order[0], 0]] if index > 1 else crossed[:1]
        hops.append(turn(after(hops[-1], *ready) if hops else hidden_states, 1))
        ready = [found[order[0], 0]] if index > 1 else []
        ready += [*hops[:1], *crossed[:1]] if index else []
        found[step, 0] = turn(after(packed[step], *ready), step)
        if index == len(order) - 1:
            ahead = [spread(cached, 0, *hops[1:2])]
        cross(hops[-1], *crossed[-1:], *packed[:1], *ahead)
    for index, step in enumerate(order):
        ready = hops[1:2] if index == 0 else []
        ready += crossed[: (index + 2) * (n_head - 1)] if index < 2 else [cached[order[0], 0]]
        swapped.append(spread(found, step, *swapped[-1:], *ready))
        if index == 0:
            ready = [found[order[min(1, groups - 2)], 0], swapped[-1]]
            cached[step, 0] = turn(after(pairs[step], *ready), step)
    for step in order[1:]:
        ready = [found[order[1], 0], *swapped[1:2], *hops[-1:]]
        cached[step, 0] = turn(after(pairs[step], *ready), step)
    ahead += [spread(cached, step, *swapped[2:3]) for step in order]
    last_step = order[-1] if order else 0
    waits = [array[step, 0] for array in (found, cached) for step in order]
    waits += crossed + swapped + ahead
    arrays, stacks = finish(found, last_step, waits, mods + [cached[last_step, 0]])
    qkv = project(mods, arrays, stacks, groups, rest, query_gain, key_gain)
    arrays, stacks = finish(cached, last_step, [cached[last_step, 0]], [])
    attention = attend(qkv, text_keys, text_values, arrays, stacks, groups, size)
    pieces = [attention[0]] + [turn(attention[step], -step) for step in range(1, groups)]
    terms = []
    for hop in range(1, n_head):
        term = combine(pieces, hop, n_head, out_weight, share, jnp.bfloat16)
        terms.append(across(term, hop))
    summed = combine(pieces, 0, n_head, out_weight, share, jnp.float32)
    for term in terms:
        summed = summed + term.astype(jnp.float32)
    return (summed * gate_mod).astype(jnp.bfloat16)


def solution(mesh):
    n_patch, n_head = mesh.shape["patch"], mesh.shape["head"]

    def whole(*arrays):
        heads = arrays[4].shape[2] // n_head // arrays[5].shape[0]
        groups = math.gcd(math.gcd(4, heads), n_patch)
        rest = n_patch // groups
        cut = Mesh(mesh.devices.reshape(groups, rest, n_head), ("group", "rest", "head"))
        patch = ("group", "rest")
        placed = (
            P(patch, "head"),
            P(),
            P(),
            P("head"),
            P(patch, None, "head"),
            P(),
            P(),
            P(None, "head"),
            P(None, "head"),
            P(patch, "head"),
            P(patch, "head"),
            P("head", None),
        )
        return jax.shard_map(
            functools.partial(per_device, groups, rest, n_head),
            mesh=cut,
            in_specs=placed,
            out_specs=P(patch, "head"),
            check_vma=False,
        )(*arrays)

    return whole
```

```python
import functools
import math

import jax
import jax.numpy as jnp
from jax import lax
from jax.experimental import pallas as pl
from jax.experimental.pallas import tpu as pltpu
from jax.sharding import Mesh
from jax.sharding import PartitionSpec as P

ANY = pl.BlockSpec(memory_space=pl.ANY)
VMEM = pl.BlockSpec(memory_space=pltpu.VMEM)
MIB = 1024 * 1024
NO_COST = pl.CostEstimate(flops=0, bytes_accessed=0, transcendentals=0)
ACROSS = (((1,), (1,)), ((), ()))


def params(limit):
    return pltpu.CompilerParams(vmem_limit_bytes=limit * MIB)


def column(index, width):
    return pl.ds(pl.multiple_of(index * width, 128), width)


def gray(place):
    return place ^ (place >> 1)


def group_at(step, groups):
    return gray(lax.rem(gray(lax.axis_index("group")) + (step + groups), groups))


def pack_kernel(groups, weight, keys, values, *refs):
    outs, sems = refs[:-1], refs[-1]
    started = []
    for step in range(groups):
        rows, pair = outs[step], outs[groups + step]
        cols = column(group_at(step, groups), rows.shape[2])
        copies = [(weight.at[:, :, cols], rows)]
        copies += [(keys.at[:, cols], pair.at[0]), (values.at[:, cols], pair.at[1])]
        for index, (source, target) in enumerate(copies):
            copy = pltpu.make_async_copy(source, target, sems.at[step, index])
            copy.start()
            started.append(copy)
    for copy in started:
        copy.wait()


def pack(weight, keys, values, groups):
    parts, depth, full = weight.shape
    tok, width = keys.shape[0], full // groups
    rows = jax.ShapeDtypeStruct((parts, depth, width), jnp.bfloat16)
    pair = jax.ShapeDtypeStruct((2, tok, width), jnp.bfloat16)
    outs = pl.pallas_call(
        functools.partial(pack_kernel, groups),
        out_shape=[rows] * groups + [pair] * groups,
        in_specs=[ANY] * 3,
        out_specs=[ANY] * (2 * groups),
        scratch_shapes=[pltpu.SemaphoreType.DMA((groups, 3))],
        compiler_params=params(4),
        cost_estimate=NO_COST,
    )(weight, keys, values)
    return outs[:groups], outs[groups:]


def stack_kernel(*refs):
    pieces, out, sems = refs[:-2], refs[-2], refs[-1]
    started = []
    for index, piece in enumerate(pieces):
        started.append(pltpu.make_async_copy(piece, out.at[index], sems.at[index]))
        started[-1].start()
    for copy in started:
        copy.wait()


def stack(pieces):
    shape = (len(pieces), *pieces[0].shape)
    return pl.pallas_call(
        stack_kernel,
        out_shape=jax.ShapeDtypeStruct(shape, pieces[0].dtype),
        in_specs=[ANY] * len(pieces),
        out_specs=ANY,
        scratch_shapes=[pltpu.SemaphoreType.DMA((len(pieces),))],
        compiler_params=params(4),
        cost_estimate=NO_COST,
    )(*pieces)


def modulate_kernel(n_head, scale, shift, *refs):
    pieces, out, rows = refs[:n_head], refs[n_head], refs[n_head + 1]
    for hop, piece in enumerate(pieces):
        part = lax.rem(lax.axis_index("head") + (n_head - hop), n_head)
        rows[:, column(part, piece.shape[1])] = piece[...].astype(jnp.float32)
    states = rows[...]
    center = jnp.mean(states, axis=-1, keepdims=True)
    apart = states - center
    spread = jnp.mean(apart * apart, axis=-1, keepdims=True)
    normed = apart * lax.rsqrt(spread + 1e-06)
    out[...] = ((1.0 + scale[...]) * normed + shift[...]).astype(jnp.bfloat16)


def modulate(pieces, scale_mod, shift_mod):
    rows, _ = pieces[0].shape
    full = scale_mod.shape[0]
    return pl.pallas_call(
        functools.partial(modulate_kernel, len(pieces)),
        out_shape=jax.ShapeDtypeStruct((rows, full), jnp.bfloat16),
        in_specs=[VMEM] * (2 + len(pieces)),
        out_specs=VMEM,
        scratch_shapes=[pltpu.VMEM((rows, full), jnp.float32)],
        compiler_params=params(12),
        cost_estimate=NO_COST,
    )(scale_mod.reshape(1, full), shift_mod.reshape(1, full), *pieces)


def project_kernel(groups, rest, n_mod, stacks, q_gain, k_gain, *refs):
    mods, arrays = refs[:n_mod], refs[n_mod : n_mod + len(stacks)]
    out, table = refs[n_mod + len(stacks) :]
    depth = arrays[0].shape[2]
    for array, keys in zip(arrays, stacks):
        for at, (step, bits) in enumerate(keys):
            patch = group_at(-step, groups) * rest + (lax.axis_index("rest") ^ bits)
            table[:, pl.ds(pl.multiple_of(patch * depth, 16), depth), :] = array[at]
    rows = jnp.concatenate([mod[...] for mod in mods], axis=0)
    size = q_gain.shape[1]
    for part in range(3):
        raw = jnp.dot(rows, table[part], preferred_element_type=jnp.float32)
        if part == 2:
            out[part] = raw.astype(jnp.bfloat16)
            continue
        gain = (q_gain, k_gain)[part][...]
        for head in range(raw.shape[1] // size):
            one = raw[:, head * size : (head + 1) * size]
            power = jnp.mean(one * one, axis=-1, keepdims=True)
            scaled = one * lax.rsqrt(power + 1e-06) * gain
            out[part, :, head * size : (head + 1) * size] = scaled.astype(jnp.bfloat16)


def project(mods, arrays, stacks, groups, rest, query_gain, key_gain):
    rows, full = mods[0].shape[0] * len(mods), mods[0].shape[1]
    width = arrays[0].shape[3]
    size = query_gain.shape[0]
    return pl.pallas_call(
        functools.partial(project_kernel, groups, rest, len(mods), stacks),
        out_shape=jax.ShapeDtypeStruct((3, rows, width), jnp.bfloat16),
        in_specs=[VMEM] * (2 + len(mods) + len(arrays)),
        out_specs=VMEM,
        scratch_shapes=[pltpu.VMEM((3, full, width), jnp.bfloat16)],
        compiler_params=params(16),
        cost_estimate=NO_COST,
    )(query_gain.reshape(1, size), key_gain.reshape(1, size), *mods, *arrays)


def attend_kernel(groups, size, stacks, qkv, text_k, text_v, *refs):
    arrays, refs = refs[: len(stacks)], refs[len(stacks) :]
    outs, scores, weights = refs[:groups], refs[groups : groups + 2], refs[groups + 2 :]
    tok, width = outs[0].shape
    text, total = text_k.shape[0], scores[0].shape[1]
    heads, many = width // size, scores[0].shape[0]
    factor = size ** (-0.5)
    mine = lax.axis_index("group")
    slots = [key for keys in stacks for key in keys]
    windows = {}
    for index, (step, bits) in enumerate(slots):
        if bits == 0:
            windows[step] = slice(text + index * tok, text + (index + 1) * tok)

    def listed(cached, which, head):
        cols = slice(head * size, (head + 1) * size)
        rows = [cached[:, column(mine * heads + head, size)]]
        for array, keys in zip(arrays, stacks):
            rows += [array[at, which, :, cols] for at in range(len(keys))]
        return jnp.concatenate(rows, axis=0)

    def spot(index):
        head, begin = index % heads, index // heads * many
        blocks = range(begin // tok, (begin + many) // tok)
        return head, slice(head * size, (head + 1) * size), begin, blocks

    def multiply(index):
        head, cols, begin, blocks = spot(index)
        held = scores[index % 2]
        held[...] = lax.dot_general(
            qkv[0, begin : begin + many, cols],
            listed(text_k, 0, head),
            ACROSS,
            preferred_element_type=jnp.float32,
        )
        for block in blocks:
            rows = slice(block * tok, (block + 1) * tok)
            held[block * tok - begin : (block + 1) * tok - begin, windows[block]] = lax.dot_general(
                qkv[0, rows, cols], qkv[1, rows, cols], ACROSS, preferred_element_type=jnp.float32
            )

    count = groups * tok // many * heads
    multiply(0)
    for index in range(count):
        if index + 1 < count:
            multiply(index + 1)
        head, cols, begin, blocks = spot(index)
        held, soft = scores[index % 2], weights[index % 2]
        for block in blocks:
            here = slice(block * tok - begin, (block + 1) * tok - begin)
            most = held[here, :size]
            for at in range(size, total, size):
                most = jnp.maximum(most, held[here, at : at + size])
            peak = jnp.max(most, axis=-1, keepdims=True)
            summed = jnp.zeros((tok, size), jnp.float32)
            for at in range(0, total, size):
                exps = jnp.exp((held[here, at : at + size] - peak) * factor)
                summed += exps
                if windows[block].start == at:
                    fresh = exps.astype(jnp.bfloat16)
                    soft[here, at : at + size] = jnp.zeros((tok, size), jnp.bfloat16)
                else:
                    soft[here, at : at + size] = exps.astype(jnp.bfloat16)
            whole = jnp.sum(summed, axis=-1, keepdims=True)
            own = qkv[2, block * tok : (block + 1) * tok, cols]
            mixed = jnp.dot(fresh, own, preferred_element_type=jnp.float32)
            mixed += jnp.dot(
                soft[here, :], listed(text_v, 1, head), preferred_element_type=jnp.float32
            )
            outs[block][:, cols] = (mixed / whole).astype(jnp.bfloat16)


def attend(qkv, text_keys, text_values, arrays, stacks, groups, size):
    _, rows, width = qkv.shape
    tok = rows // groups
    total = text_keys.shape[0] + tok * sum(len(keys) for keys in stacks)
    many = tok * (2 if groups % 2 == 0 else 1)
    return pl.pallas_call(
        functools.partial(attend_kernel, groups, size, stacks),
        out_shape=[jax.ShapeDtypeStruct((tok, width), jnp.bfloat16)] * groups,
        in_specs=[VMEM] * (3 + len(arrays)),
        out_specs=[VMEM] * groups,
        scratch_shapes=[
            pltpu.VMEM((many, total), jnp.float32),
            pltpu.VMEM((many, total), jnp.float32),
            pltpu.VMEM((many, total), jnp.bfloat16),
            pltpu.VMEM((many, total), jnp.bfloat16),
        ],
        compiler_params=params(24),
        cost_estimate=NO_COST,
    )(qkv, text_keys, text_values, *arrays)


def combine_kernel(hop, n_head, weight, *refs):
    pieces, out, rows = refs[:-2], refs[-2], refs[-1]
    wide = pieces[0].shape[1]
    for step, piece in enumerate(pieces):
        rows[:, column(group_at(step, len(pieces)), wide)] = piece[...]
    side = lax.rem(lax.axis_index("head") + hop, n_head)
    table = weight[:, column(side, out.shape[1])]
    out[...] = jnp.dot(rows[...], table, preferred_element_type=jnp.float32).astype(out.dtype)


def combine(pieces, hop, n_head, weight, share, kind):
    tok = pieces[0].shape[0]
    depth = weight.shape[0]
    return pl.pallas_call(
        functools.partial(combine_kernel, hop, n_head),
        out_shape=jax.ShapeDtypeStruct((tok, share), kind),
        in_specs=[VMEM] * (1 + len(pieces)),
        out_specs=VMEM,
        scratch_shapes=[pltpu.VMEM((tok, depth), jnp.bfloat16)],
        compiler_params=params(6),
        cost_estimate=NO_COST,
    )(weight, *pieces)


def after(array, *others):
    return lax.optimization_barrier((array, *others))[0] if others else array


def per_device(
    groups,
    rest,
    n_head,
    hidden_states,
    shift_mod,
    scale_mod,
    gate_mod,
    qkv_weight,
    query_gain,
    key_gain,
    text_keys,
    text_values,
    stale_keys,
    stale_values,
    out_weight,
):
    tok, share = hidden_states.shape
    size = query_gain.shape[0]

    def turn(array, step):
        pairs = [(i, gray((gray(i) + step) % groups)) for i in range(groups)]
        return lax.ppermute(array, "group", pairs)

    def swap(array, bit):
        return lax.ppermute(array, "rest", [(i, i ^ bit) for i in range(rest)])

    def across(array, hop):
        return lax.ppermute(array, "head", [(i, (i + hop) % n_head) for i in range(n_head)])

    def spread(found, step, *ready):
        bit = rest // 2
        while bit > 1:
            for (mark, bits), piece in list(found.items()):
                if mark == step:
                    found[step, bits | bit] = swap(after(piece, *ready), bit)
            bit //= 2
        return found[step, max(bits for mark, bits in found if mark == step)]

    def finish(found, last_step, early_waits, late_waits):
        names = list(found)
        stacks = [[name] for name in names]
        arrays = [found[name][None] for name in names]
        if rest % 2 == 0:
            early = [name for name in names if name[0] != last_step]
            late = [name for name in names if name[0] == last_step]
            for part, waits in ((early, early_waits), (late, late_waits)):
                if not part:
                    continue
                pieces = [found[name] for name in part]
                pieces[0] = after(pieces[0], *waits)
                joined = stack(pieces) if len(part) > 1 else pieces[0][None]
                arrays.append(swap(joined, 1))
                stacks.append([(step, bits | 1) for step, bits in part])
        return arrays, stacks

    packed, pairs = pack(jnp.transpose(qkv_weight, (1, 0, 2)), stale_keys, stale_values, groups)
    found, cached = {(0, 0): packed[0]}, {(0, 0): pairs[0]}
    mods, hops, crossed, swapped = [], [], [], []

    def cross(piece, *ready):
        slices = [piece]
        for hop in range(1, n_head):
            slices.append(across(after(piece, *ready), hop))
            crossed.append(slices[-1])
        mods.append(modulate(slices, scale_mod, shift_mod))

    cross(hidden_states)
    swapped.append(spread(found, 0))
    ahead = []
    order = [1, *range(groups - 1, 1, -1)][: groups - 1]
    for index, step in enumerate(order):
        ready = [found[order[0], 0]] if index > 1 else crossed[:1]
        hops.append(turn(after(hops[-1], *ready) if hops else hidden_states, 1))
        ready = [found[order[0], 0]] if index > 1 else []
        ready += [*hops[:1], *crossed[:1]] if index else []
        found[step, 0] = turn(after(packed[step], *ready), step)
        if index == len(order) - 1:
            ahead = [spread(cached, 0, *hops[1:2], *mods[:2])]
        cross(hops[-1], *crossed[-1:], *packed[:1], *ahead)
    for index, step in enumerate(order):
        ready = hops[1:2] if index == 0 else []
        ready += crossed[: (index + 2) * (n_head - 1)] if index < 2 else [cached[order[0], 0]]
        swapped.append(spread(found, step, *swapped[-1:], *ready))
        if index == 0:
            ready = [found[order[min(1, groups - 2)], 0], swapped[-1]]
            cached[step, 0] = turn(after(pairs[step], *ready), step)
    for step in order[1:]:
        ready = [found[order[1], 0], *swapped[1:2], *hops[-1:]]
        cached[step, 0] = turn(after(pairs[step], *ready), step)
    ahead += [spread(cached, step, *swapped[2:3]) for step in order]
    last_step = order[-1] if order else 0
    waits = [array[step, 0] for array in (found, cached) for step in order]
    waits += crossed + swapped + ahead
    arrays, stacks = finish(found, last_step, waits, mods + [cached[last_step, 0]])
    qkv = project(mods, arrays, stacks, groups, rest, query_gain, key_gain)
    arrays, stacks = finish(cached, last_step, [cached[last_step, 0]], [])
    attention = attend(qkv, text_keys, text_values, arrays, stacks, groups, size)
    pieces = [attention[0]] * groups
    for step in sorted(range(1, groups), key=lambda step: -min(step, groups - step)):
        pieces[step] = turn(attention[step], -step)
    terms = []
    for hop in range(1, n_head):
        term = combine(pieces, hop, n_head, out_weight, share, jnp.bfloat16)
        terms.append(across(term, hop))
    summed = combine(pieces, 0, n_head, out_weight, share, jnp.float32)
    for term in terms:
        summed = summed + term.astype(jnp.float32)
    return (summed * gate_mod).astype(jnp.bfloat16)


def solution(mesh):
    n_patch, n_head = mesh.shape["patch"], mesh.shape["head"]

    def whole(*arrays):
        heads = arrays[4].shape[2] // n_head // arrays[5].shape[0]
        groups = math.gcd(math.gcd(4, heads), n_patch)
        rest = n_patch // groups
        cut = Mesh(mesh.devices.reshape(groups, rest, n_head), ("group", "rest", "head"))
        patch = ("group", "rest")
        placed = (
            P(patch, "head"),
            P(),
            P(),
            P("head"),
            P(patch, None, "head"),
            P(),
            P(),
            P(None, "head"),
            P(None, "head"),
            P(patch, "head"),
            P(patch, "head"),
            P("head", None),
        )
        return jax.shard_map(
            functools.partial(per_device, groups, rest, n_head),
            mesh=cut,
            in_specs=placed,
            out_specs=P(patch, "head"),
            check_vma=False,
        )(*arrays)

    return whole
```

```python
import functools
import math

import jax
import jax.numpy as jnp
from jax import lax
from jax.experimental import pallas as pl
from jax.experimental.pallas import tpu as pltpu
from jax.sharding import Mesh
from jax.sharding import PartitionSpec as P

ANY = pl.BlockSpec(memory_space=pl.ANY)
VMEM = pl.BlockSpec(memory_space=pltpu.VMEM)
MIB = 1024 * 1024
NO_COST = pl.CostEstimate(flops=0, bytes_accessed=0, transcendentals=0)
ACROSS = (((1,), (1,)), ((), ()))


def params(limit):
    return pltpu.CompilerParams(vmem_limit_bytes=limit * MIB)


def column(index, width):
    return pl.ds(pl.multiple_of(index * width, 128), width)


def gray(place):
    return place ^ (place >> 1)


def group_at(step, groups):
    return gray(lax.rem(gray(lax.axis_index("group")) + (step + groups), groups))


def pack_kernel(groups, weight, keys, values, *refs):
    outs, sems = refs[:-1], refs[-1]
    started = []
    for step in range(groups):
        rows, pair = outs[step], outs[groups + step]
        cols = column(group_at(step, groups), rows.shape[2])
        copies = [(weight.at[:, :, cols], rows)]
        copies += [(keys.at[:, cols], pair.at[0]), (values.at[:, cols], pair.at[1])]
        for index, (source, target) in enumerate(copies):
            copy = pltpu.make_async_copy(source, target, sems.at[step, index])
            copy.start()
            started.append(copy)
    for copy in started:
        copy.wait()


def pack(weight, keys, values, groups):
    parts, depth, full = weight.shape
    tok, width = keys.shape[0], full // groups
    rows = jax.ShapeDtypeStruct((parts, depth, width), jnp.bfloat16)
    pair = jax.ShapeDtypeStruct((2, tok, width), jnp.bfloat16)
    outs = pl.pallas_call(
        functools.partial(pack_kernel, groups),
        out_shape=[rows] * groups + [pair] * groups,
        in_specs=[ANY] * 3,
        out_specs=[ANY] * (2 * groups),
        scratch_shapes=[pltpu.SemaphoreType.DMA((groups, 3))],
        compiler_params=params(4),
        cost_estimate=NO_COST,
    )(weight, keys, values)
    return outs[:groups], outs[groups:]


def stack_kernel(*refs):
    pieces, out, sems = refs[:-2], refs[-2], refs[-1]
    started = []
    for index, piece in enumerate(pieces):
        started.append(pltpu.make_async_copy(piece, out.at[index], sems.at[index]))
        started[-1].start()
    for copy in started:
        copy.wait()


def stack(pieces):
    shape = (len(pieces), *pieces[0].shape)
    return pl.pallas_call(
        stack_kernel,
        out_shape=jax.ShapeDtypeStruct(shape, pieces[0].dtype),
        in_specs=[ANY] * len(pieces),
        out_specs=ANY,
        scratch_shapes=[pltpu.SemaphoreType.DMA((len(pieces),))],
        compiler_params=params(4),
        cost_estimate=NO_COST,
    )(*pieces)


def modulate_kernel(n_head, scale, shift, *refs):
    pieces, out, rows = refs[:n_head], refs[n_head], refs[n_head + 1]
    for hop, piece in enumerate(pieces):
        part = lax.rem(lax.axis_index("head") + (n_head - hop), n_head)
        rows[:, column(part, piece.shape[1])] = piece[...].astype(jnp.float32)
    states = rows[...]
    center = jnp.mean(states, axis=-1, keepdims=True)
    apart = states - center
    spread = jnp.mean(apart * apart, axis=-1, keepdims=True)
    normed = apart * lax.rsqrt(spread + 1e-06)
    out[...] = ((1.0 + scale[...]) * normed + shift[...]).astype(jnp.bfloat16)


def modulate(pieces, scale_mod, shift_mod):
    rows, _ = pieces[0].shape
    full = scale_mod.shape[0]
    return pl.pallas_call(
        functools.partial(modulate_kernel, len(pieces)),
        out_shape=jax.ShapeDtypeStruct((rows, full), jnp.bfloat16),
        in_specs=[VMEM] * (2 + len(pieces)),
        out_specs=VMEM,
        scratch_shapes=[pltpu.VMEM((rows, full), jnp.float32)],
        compiler_params=params(12),
        cost_estimate=NO_COST,
    )(scale_mod.reshape(1, full), shift_mod.reshape(1, full), *pieces)


def project_kernel(groups, rest, n_mod, stacks, q_gain, k_gain, *refs):
    mods, arrays = refs[:n_mod], refs[n_mod : n_mod + len(stacks)]
    out, table = refs[n_mod + len(stacks) :]
    depth = arrays[0].shape[2]
    for array, keys in zip(arrays, stacks):
        for at, (step, bits) in enumerate(keys):
            patch = group_at(-step, groups) * rest + (lax.axis_index("rest") ^ bits)
            table[:, pl.ds(pl.multiple_of(patch * depth, 16), depth), :] = array[at]
    rows = jnp.concatenate([mod[...] for mod in mods], axis=0)
    size = q_gain.shape[1]
    for part in range(3):
        raw = jnp.dot(rows, table[part], preferred_element_type=jnp.float32)
        if part == 2:
            out[part] = raw.astype(jnp.bfloat16)
            continue
        gain = (q_gain, k_gain)[part][...]
        for head in range(raw.shape[1] // size):
            one = raw[:, head * size : (head + 1) * size]
            power = jnp.mean(one * one, axis=-1, keepdims=True)
            scaled = one * lax.rsqrt(power + 1e-06) * gain
            out[part, :, head * size : (head + 1) * size] = scaled.astype(jnp.bfloat16)


def project(mods, arrays, stacks, groups, rest, query_gain, key_gain):
    rows, full = mods[0].shape[0] * len(mods), mods[0].shape[1]
    width = arrays[0].shape[3]
    size = query_gain.shape[0]
    return pl.pallas_call(
        functools.partial(project_kernel, groups, rest, len(mods), stacks),
        out_shape=jax.ShapeDtypeStruct((3, rows, width), jnp.bfloat16),
        in_specs=[VMEM] * (2 + len(mods) + len(arrays)),
        out_specs=VMEM,
        scratch_shapes=[pltpu.VMEM((3, full, width), jnp.bfloat16)],
        compiler_params=params(16),
        cost_estimate=NO_COST,
    )(query_gain.reshape(1, size), key_gain.reshape(1, size), *mods, *arrays)


def attend_kernel(groups, size, stacks, qkv, text_k, text_v, *refs):
    arrays, refs = refs[: len(stacks)], refs[len(stacks) :]
    outs, scores, weights = refs[:groups], refs[groups : groups + 2], refs[groups + 2 :]
    tok, width = outs[0].shape
    text, total = text_k.shape[0], scores[0].shape[1]
    heads, many = width // size, scores[0].shape[0]
    factor = size ** (-0.5)
    mine = lax.axis_index("group")
    slots = [key for keys in stacks for key in keys]
    windows = {}
    for index, (step, bits) in enumerate(slots):
        if bits == 0:
            windows[step] = slice(text + index * tok, text + (index + 1) * tok)

    def listed(cached, which, head):
        cols = slice(head * size, (head + 1) * size)
        rows = [cached[:, column(mine * heads + head, size)]]
        for array, keys in zip(arrays, stacks):
            rows += [array[at, which, :, cols] for at in range(len(keys))]
        return jnp.concatenate(rows, axis=0)

    def spot(index):
        head, begin = index % heads, index // heads * many
        blocks = range(begin // tok, (begin + many) // tok)
        return head, slice(head * size, (head + 1) * size), begin, blocks

    def multiply(index):
        head, cols, begin, blocks = spot(index)
        held = scores[index % 2]
        held[...] = lax.dot_general(
            qkv[0, begin : begin + many, cols],
            listed(text_k, 0, head),
            ACROSS,
            preferred_element_type=jnp.float32,
        )
        for block in blocks:
            rows = slice(block * tok, (block + 1) * tok)
            held[block * tok - begin : (block + 1) * tok - begin, windows[block]] = lax.dot_general(
                qkv[0, rows, cols], qkv[1, rows, cols], ACROSS, preferred_element_type=jnp.float32
            )

    count = groups * tok // many * heads
    multiply(0)
    for index in range(count):
        if index + 1 < count:
            multiply(index + 1)
        head, cols, begin, blocks = spot(index)
        held, soft = scores[index % 2], weights[index % 2]
        for block in blocks:
            here = slice(block * tok - begin, (block + 1) * tok - begin)
            most = held[here, :size]
            for at in range(size, total, size):
                most = jnp.maximum(most, held[here, at : at + size])
            peak = jnp.max(most, axis=-1, keepdims=True)
            summed = jnp.zeros((tok, size), jnp.float32)
            for at in range(0, total, size):
                exps = jnp.exp((held[here, at : at + size] - peak) * factor)
                summed += exps
                if windows[block].start == at:
                    fresh = exps.astype(jnp.bfloat16)
                    soft[here, at : at + size] = jnp.zeros((tok, size), jnp.bfloat16)
                else:
                    soft[here, at : at + size] = exps.astype(jnp.bfloat16)
            whole = jnp.sum(summed, axis=-1, keepdims=True)
            own = qkv[2, block * tok : (block + 1) * tok, cols]
            mixed = jnp.dot(fresh, own, preferred_element_type=jnp.float32)
            mixed += jnp.dot(
                soft[here, :], listed(text_v, 1, head), preferred_element_type=jnp.float32
            )
            outs[block][:, cols] = (mixed / whole).astype(jnp.bfloat16)


def attend(qkv, text_keys, text_values, arrays, stacks, groups, size):
    _, rows, width = qkv.shape
    tok = rows // groups
    total = text_keys.shape[0] + tok * sum(len(keys) for keys in stacks)
    many = tok * (2 if groups % 2 == 0 else 1)
    return pl.pallas_call(
        functools.partial(attend_kernel, groups, size, stacks),
        out_shape=[jax.ShapeDtypeStruct((tok, width), jnp.bfloat16)] * groups,
        in_specs=[VMEM] * (3 + len(arrays)),
        out_specs=[VMEM] * groups,
        scratch_shapes=[
            pltpu.VMEM((many, total), jnp.float32),
            pltpu.VMEM((many, total), jnp.float32),
            pltpu.VMEM((many, total), jnp.bfloat16),
            pltpu.VMEM((many, total), jnp.bfloat16),
        ],
        compiler_params=params(24),
        cost_estimate=NO_COST,
    )(qkv, text_keys, text_values, *arrays)


def combine_kernel(hop, n_head, weight, *refs):
    pieces, out, rows = refs[:-2], refs[-2], refs[-1]
    wide = pieces[0].shape[1]
    for step, piece in enumerate(pieces):
        rows[:, column(group_at(step, len(pieces)), wide)] = piece[...]
    side = lax.rem(lax.axis_index("head") + hop, n_head)
    table = weight[:, column(side, out.shape[1])]
    out[...] = jnp.dot(rows[...], table, preferred_element_type=jnp.float32).astype(out.dtype)


def combine(pieces, hop, n_head, weight, share, kind):
    tok = pieces[0].shape[0]
    depth = weight.shape[0]
    return pl.pallas_call(
        functools.partial(combine_kernel, hop, n_head),
        out_shape=jax.ShapeDtypeStruct((tok, share), kind),
        in_specs=[VMEM] * (1 + len(pieces)),
        out_specs=VMEM,
        scratch_shapes=[pltpu.VMEM((tok, depth), jnp.bfloat16)],
        compiler_params=params(6),
        cost_estimate=NO_COST,
    )(weight, *pieces)


def after(array, *others):
    return lax.optimization_barrier((array, *others))[0] if others else array


def per_device(
    groups,
    rest,
    n_head,
    hidden_states,
    shift_mod,
    scale_mod,
    gate_mod,
    qkv_weight,
    query_gain,
    key_gain,
    text_keys,
    text_values,
    stale_keys,
    stale_values,
    out_weight,
):
    tok, share = hidden_states.shape
    size = query_gain.shape[0]

    def turn(array, step):
        pairs = [(i, gray((gray(i) + step) % groups)) for i in range(groups)]
        return lax.ppermute(array, "group", pairs)

    def swap(array, bit):
        return lax.ppermute(array, "rest", [(i, i ^ bit) for i in range(rest)])

    def across(array, hop):
        return lax.ppermute(array, "head", [(i, (i + hop) % n_head) for i in range(n_head)])

    def spread(found, step, *ready):
        bit = rest // 2
        while bit > 1:
            for (mark, bits), piece in list(found.items()):
                if mark == step:
                    found[step, bits | bit] = swap(after(piece, *ready), bit)
            bit //= 2
        return found[step, max(bits for mark, bits in found if mark == step)]

    def finish(found, last_step, early_waits, late_waits):
        names = list(found)
        stacks = [[name] for name in names]
        arrays = [found[name][None] for name in names]
        if rest % 2 == 0:
            early = [name for name in names if name[0] != last_step]
            late = [name for name in names if name[0] == last_step]
            for part, waits in ((early, early_waits), (late, late_waits)):
                if not part:
                    continue
                pieces = [found[name] for name in part]
                pieces[0] = after(pieces[0], *waits)
                joined = stack(pieces) if len(part) > 1 else pieces[0][None]
                arrays.append(swap(joined, 1))
                stacks.append([(step, bits | 1) for step, bits in part])
        return arrays, stacks

    packed, pairs = pack(jnp.transpose(qkv_weight, (1, 0, 2)), stale_keys, stale_values, groups)
    found, cached = {(0, 0): packed[0]}, {(0, 0): pairs[0]}
    mods, hops, crossed, swapped = [], [], [], []

    def cross(piece, *ready):
        slices = [piece]
        for hop in range(1, n_head):
            slices.append(across(after(piece, *ready), hop))
            crossed.append(slices[-1])
        mods.append(modulate(slices, scale_mod, shift_mod))

    cross(hidden_states)
    swapped.append(spread(found, 0))
    ahead = []
    order = [1, *range(groups - 1, 1, -1)][: groups - 1]
    for index, step in enumerate(order):
        ready = [found[order[0], 0]] if index > 1 else crossed[:1]
        hops.append(turn(after(hops[-1], *ready) if hops else hidden_states, 1))
        ready = [found[order[0], 0]] if index > 1 else []
        ready += [*hops[:1], *crossed[:1]] if index else []
        found[step, 0] = turn(after(packed[step], *ready), step)
        if index == len(order) - 1:
            ahead = [spread(cached, 0, *hops[1:2], *mods[:3])]
        cross(hops[-1], *crossed[-1:], *packed[:1], *ahead)
    for index, step in enumerate(order):
        ready = hops[1:2] if index == 0 else []
        ready += crossed[: (index + 2) * (n_head - 1)] if index < 2 else [cached[order[0], 0]]
        swapped.append(spread(found, step, *swapped[-1:], *ready))
        if index == 0:
            ready = [found[order[min(1, groups - 2)], 0], swapped[-1]]
            cached[step, 0] = turn(after(pairs[step], *ready), step)
    for step in order[1:]:
        ready = [found[order[1], 0], *swapped[1:2], *hops[-1:]]
        cached[step, 0] = turn(after(pairs[step], *ready), step)
    ahead += [spread(cached, step, *swapped[2:3]) for step in order]
    last_step = order[-1] if order else 0
    waits = [array[step, 0] for array in (found, cached) for step in order]
    waits += crossed + swapped + ahead
    arrays, stacks = finish(found, last_step, waits, mods + [cached[last_step, 0]])
    qkv = project(mods, arrays, stacks, groups, rest, query_gain, key_gain)
    arrays, stacks = finish(cached, last_step, [cached[last_step, 0], arrays[-1]], [])
    attention = attend(qkv, text_keys, text_values, arrays, stacks, groups, size)
    pieces = [attention[0]] * groups
    for step in sorted(range(1, groups), key=lambda step: -min(step, groups - step)):
        pieces[step] = turn(attention[step], -step)
    terms = []
    for hop in range(1, n_head):
        term = combine(pieces, hop, n_head, out_weight, share, jnp.bfloat16)
        terms.append(across(term, hop))
    summed = combine(pieces, 0, n_head, out_weight, share, jnp.float32)
    for term in terms:
        summed = summed + term.astype(jnp.float32)
    return (summed * gate_mod).astype(jnp.bfloat16)


def solution(mesh):
    n_patch, n_head = mesh.shape["patch"], mesh.shape["head"]

    def whole(*arrays):
        heads = arrays[4].shape[2] // n_head // arrays[5].shape[0]
        groups = math.gcd(math.gcd(4, heads), n_patch)
        rest = n_patch // groups
        cut = Mesh(mesh.devices.reshape(groups, rest, n_head), ("group", "rest", "head"))
        patch = ("group", "rest")
        placed = (
            P(patch, "head"),
            P(),
            P(),
            P("head"),
            P(patch, None, "head"),
            P(),
            P(),
            P(None, "head"),
            P(None, "head"),
            P(patch, "head"),
            P(patch, "head"),
            P("head", None),
        )
        return jax.shard_map(
            functools.partial(per_device, groups, rest, n_head),
            mesh=cut,
            in_specs=placed,
            out_specs=P(patch, "head"),
            check_vma=False,
        )(*arrays)

    return whole
```
